512 devices in a mesh: rep: 64 (over x, z_hi, y), tp: 8 (over z_lo, core).
Axes of the slice: x: 4, y: 8, z: 8 (z_hi: 2, z_lo: 4; z = z_hi * 4 + z_lo), core: 2. Of those that a mesh axis runs over, the one named last changes fastest.
Arguments:
- weight: bfloat16 [64, 2048, 2048], P('rep', None, 'tp'), may hold values from -6 to 6
- second_moment: bfloat16 [64, 2048, 2048], P('rep', None, 'tp'), may hold values from 0.0009994507 to 1
- inputs: bfloat16 [2, 64, 1024, 2048], P(None, 'rep', 'tp'), may hold values from -6 to 6
- cotangent: bfloat16 [2, 64, 1024, 2048], P(None, 'rep', None, 'tp'), may hold values from -6 to 6
- gossip_steps: int32 [2], replicated, may hold values from 0 to 5, as said below
Outputs:
- averaged: bfloat16 [64, 2048, 2048], P('rep', None, 'tp')
The draws below stay inside these ranges and needn't reach their ends.
Inputs may be any that keep to these rules, and one draw needn't show every extreme that they name: `gossip_steps`: the two entries differ; one of them is 5.
All inputs are finite; a program needn't handle non-finite values.
Results may differ from the reference program's by a relative error of at most 0.015.
Values may be sent and summed in bfloat16 or wider, within the bound.
A program may use at most 64 MiB of HBM per device.

```python
import math
import jax
import jax.numpy as jnp
from jax import lax

DIN = 2048
DOUT = 2048
STEPS = 2
ROWS = 1024
REPS = 64
REP_BITS = 6
N_REP = 64


def draw_gossip_steps(key, part):
    key = jax.random.fold_in(key, 7)
    order_key, lower_key = jax.random.split(key)
    highest = jnp.int32(REP_BITS - 1)
    lower = jax.random.randint(lower_key, (), 0, REP_BITS - 1).astype(jnp.int32)
    order = jax.random.randint(order_key, (), 0, 2)
    first = jnp.where(order == 0, highest, lower)
    second = jnp.where(order == 0, lower, highest)
    return jnp.stack([first, second]).astype(jnp.int32)


def block_scale(stream_key, extent, shards, least, largest):
    level, own = 1.0, jax.random.fold_in(stream_key, 6)
    for axis_at, blocks in shards:
        steps = jnp.exp(jax.random.uniform(jax.random.fold_in(own, axis_at), (blocks,), jnp.float32, least / len(shards), largest / len(shards)))
        level = level * jnp.repeat(steps, extent[axis_at] // blocks).reshape([-1 if axis == axis_at else 1 for axis in range(len(extent))])
    return level


def normal_values(rng, extent, scale, reach, cuts=(), kind=jnp.bfloat16):
    result = jax.random.normal(rng, extent, jnp.float32) * scale
    if len(cuts) > 0:
        result = block_scale(rng, extent, cuts, -0.22, 0.18) * result
    return jnp.clip(result, min=-reach, max=reach).astype(kind)


def setup_inputs(seed: int = 0) -> dict:
    key_of = jax.random.split(jax.random.key(seed), 6)
    return {
        "weight": normal_values(key_of[0], (REPS, DIN, DOUT), 1.0, 6.0, ((0, 64), (2, 8))),
        "second_moment": jnp.clip(jnp.exp(math.log(1.0) - 6.9083047 * jax.random.uniform(key_of[1], (REPS, DIN, DOUT), jnp.float32) ** block_scale(key_of[1], (REPS, DIN, DOUT), ((0, 64), (2, 8)), -0.2, 0.2)), 0.0009994507, 1.0).astype(jnp.bfloat16),
        "inputs": normal_values(key_of[2], (STEPS, REPS, ROWS, DIN), 1.0, 6.0, ((1, 64), (2, 8))),
        "cotangent": normal_values(key_of[3], (STEPS, REPS, ROWS, DOUT), 1.0, 6.0, ((1, 64), (3, 8))),
        "gossip_steps": draw_gossip_steps(jax.random.fold_in(key_of[5], 71), 0),
    }


def adam_update(weight, first, second, grad):
    first_new = 0.9 * first.astype(jnp.float32) + 0.1 * grad
    second_new = 0.95 * second.astype(jnp.float32) + 0.05 * grad * grad
    moved = weight.astype(jnp.float32) - 0.2 * first_new / (jnp.sqrt(second_new) + 1e-08)
    return (moved.astype(jnp.bfloat16), first_new.astype(jnp.bfloat16), second_new.astype(jnp.bfloat16))

def reference(weight, second_moment, inputs, cotangent, gossip_steps):
    factor = 1.0 / math.sqrt(DIN)
    first_moment = jnp.zeros_like(weight)

    def one_replica(operands):
        tensor, first, second, acts, back = operands
        grad = jnp.dot(acts.T, back, preferred_element_type=jnp.float32) * factor
        return adam_update(tensor, first, second, grad)
    for step in range(STEPS):
        weight, first_moment, second_moment = lax.map(one_replica, (weight, first_moment, second_moment, inputs[step], cotangent[step]))
        partner = jnp.bitwise_xor(jnp.arange(N_REP, dtype=jnp.int32), jnp.left_shift(jnp.int32(1), gossip_steps[step]))
        other = jnp.take(weight, partner, axis=0)
        weight = ((weight.astype(jnp.float32) + other.astype(jnp.float32)) * 0.5).astype(jnp.bfloat16)
    return weight
```

```python
from functools import partial
import math

import jax
import jax.numpy as jnp
from jax import lax
from jax.experimental import pallas as pl
from jax.experimental.pallas import tpu as pltpu
from jax.sharding import PartitionSpec as P

CHUNKS = 8
FULL = 2
LAG = 2
LAST = 1
AHEAD = 4
TILE = 64
MESH = pl.DeviceIdType.MESH


def gossip_kernel(
    bit_a,
    bit_b,
    w_hbm,
    v_hbm,
    x_hbm,
    c_hbm,
    o_hbm,
    xall,
    w_own,
    v_own,
    c_own,
    c_end,
    grad,
    first,
    u0,
    u0_in,
    u1,
    u1_in,
    out,
    p_out,
    p_in,
    sem_in,
    sem_x,
    recv_n,
    recv_s,
    send_r,
    send_l,
    send_s,
    sem_a,
    sem_b,
    sem_p,
    sem_c,
    sem_o,
):
    rows = x_hbm.shape[2]
    din = x_hbm.shape[3]
    width = xall.shape[3]
    total = xall.shape[2]
    chip_rows = 2 * rows
    rest = total - chip_rows
    factor = 1.0 / math.sqrt(din)

    rep = lax.axis_index("rep")
    tp = lax.axis_index("tp")
    z = tp // 2
    core = tp % 2
    sibling = {"tp": z * 2 + 1 - core}
    right = {"tp": jnp.minimum(tp + 2, 7)}
    left = {"tp": jnp.maximum(tp - 2, 0)}
    at_a, at_b = 1 << bit_a, 1 << bit_b
    mate_a = {"rep": rep + at_a - 2 * at_a * ((rep // at_a) % 2)}
    mate_b = {"rep": rep + at_b - 2 * at_b * ((rep // at_b) % 2)}
    is_first = z == 0
    is_last = z == 3
    is_end = jnp.logical_or(is_first, is_last)
    is_mid = jnp.logical_not(is_end)
    inner = {"tp": jnp.where(is_first, 2 + core, 4 + core)}
    outer = {"tp": jnp.where(z == 1, core, 6 + core)}

    x_rows = pl.ds(pl.multiple_of(tp * rows, rows), rows)

    def load_x(s, k):
        cols = pl.ds(pl.multiple_of(k * width, width), width)
        return pltpu.make_async_copy(
            x_hbm.at[s, 0, :, cols], xall.at[s, k, x_rows, :], sem_x.at[s, k]
        )

    loads = [
        pltpu.make_async_copy(c_hbm.at[:, 0], c_own, sem_in.at[0]),
        pltpu.make_async_copy(w_hbm.at[0], w_own, sem_in.at[1]),
        pltpu.make_async_copy(v_hbm.at[0], v_own, sem_in.at[2]),
    ]

    def start_x(k, carry):
        load_x(0, k).start()
        load_x(1, k).start()
        return carry

    lax.fori_loop(0, CHUNKS, start_x, 0)
    for load in loads:
        load.start()

    barrier = pltpu.get_barrier_semaphore()
    for mate in (sibling, mate_a, mate_b):
        pl.semaphore_signal(barrier, inc=1, device_id=mate, device_id_type=MESH)

    @pl.when(z < 3)
    def _():
        pl.semaphore_signal(barrier, inc=1, device_id=right, device_id_type=MESH)

    @pl.when(z > 0)
    def _():
        pl.semaphore_signal(barrier, inc=1, device_id=left, device_id_type=MESH)

    pl.semaphore_wait(barrier, jnp.where(is_end, 4, 5))

    def block(s, k, source):
        at = pl.ds(pl.multiple_of((source * 2 + core) * rows, rows), rows)
        return xall.at[s, k, at, :]

    def hop(s, k, source, send, recv, to):
        return pltpu.make_async_remote_copy(
            src_ref=block(s, k, source),
            dst_ref=block(s, k, source),
            send_sem=send.at[source, s, k],
            recv_sem=recv.at[source, s, k],
            device_id=to,
            device_id_type=MESH,
        )

    def to_right(s, k, source):
        return hop(s, k, source, send_r, recv_n, right)

    def to_left(s, k, source):
        return hop(s, k, source, send_l, recv_n, left)

    def to_sibling(s, k, source):
        return hop(s, k, source, send_s, recv_s, sibling)

    def goes_right(k):
        return jnp.logical_or(z < 2, jnp.logical_and(z == 2, k < FULL))

    def goes_left(k):
        return jnp.logical_or(z > 1, jnp.logical_and(z == 1, k < FULL))

    def gathers(k):
        return jnp.logical_or(is_mid, k < FULL)

    def give_c(s):
        at = pl.ds(pl.multiple_of(jnp.where(is_first, chip_rows, 0), chip_rows), rest)
        return pltpu.make_async_remote_copy(
            src_ref=c_hbm.at[s, 0, at, :],
            dst_ref=c_end.at[s],
            send_sem=sem_c.at[0, s],
            recv_sem=sem_c.at[1, s],
            device_id=inner,
            device_id_type=MESH,
        )

    def give_p(s, k):
        return pltpu.make_async_remote_copy(
            src_ref=p_out.at[s, k],
            dst_ref=p_in.at[s, k],
            send_sem=sem_p.at[0, s, k],
            recv_sem=sem_p.at[1, s, k],
            device_id=outer,
            device_id_type=MESH,
        )

    def swap(k, mine, theirs, sems, mate):
        return pltpu.make_async_remote_copy(
            src_ref=mine.at[k],
            dst_ref=theirs.at[k],
            send_sem=sems.at[0, k],
            recv_sem=sems.at[1, k],
            device_id=mate,
            device_id_type=MESH,
        )

    def swap_a(k):
        return swap(k, u0, u0_in, sem_a, mate_a)

    def swap_b(k):
        return swap(k, u1, u1_in, sem_b, mate_b)

    def store(k):
        at = pl.ds(pl.multiple_of(k * width, width), width)
        return pltpu.make_async_copy(out.at[k], o_hbm.at[0, at, :], sem_o.at[k])

    def send_own(s, k):
        load_x(s, k).wait()

        @pl.when(goes_right(k))
        def _():
            to_right(s, k, z).start()

        @pl.when(goes_left(k))
        def _():
            to_left(s, k, z).start()

        to_sibling(s, k, z).start()

    def pass_on(apart, s, k):
        @pl.when(jnp.logical_and(z >= apart, gathers(k)))
        def _():
            source = z - apart
            to_right(s, k, source).wait_recv()

            @pl.when(goes_right(k))
            def _():
                to_right(s, k, source).start()

            to_sibling(s, k, source).start()

        @pl.when(jnp.logical_and(z + apart <= 3, gathers(k)))
        def _():
            source = z + apart
            to_left(s, k, source).wait_recv()

            @pl.when(goes_left(k))
            def _():
                to_left(s, k, source).start()

            to_sibling(s, k, source).start()

    def drain(s, k):
        for source in range(4):
            has = jnp.logical_or(z == source, gathers(k))

            @pl.when(jnp.logical_and(z >= source, jnp.logical_and(has, goes_right(k))))
            def _():
                to_right(s, k, source).wait_send()

            @pl.when(jnp.logical_and(z <= source, jnp.logical_and(has, goes_left(k))))
            def _():
                to_left(s, k, source).wait_send()

            @pl.when(has)
            def _():
                to_sibling(s, k, source).wait_send()

        @pl.when(jnp.logical_and(is_mid, k >= FULL))
        def _():
            give_p(s, k).wait_send()

    def product(x, c):
        return lax.dot_general(
            x, c, (((0,), (0,)), ((), ())), preferred_element_type=jnp.float32
        )

    def gradient(s, k):
        for source in range(4):

            @pl.when(jnp.logical_or(z == source, gathers(k)))
            def _():
                to_sibling(s, k, source).wait_recv()

        @pl.when(jnp.logical_and(is_mid, k >= FULL))
        def _():
            @pl.when(k == FULL)
            def _():
                give_c(s).wait_recv()

            at = pl.ds(pl.multiple_of(jnp.where(z == 1, chip_rows, 0), chip_rows), rest)
            p_out[s, k] = product(xall[s, k, at, :], c_end[s]).astype(jnp.bfloat16)
            give_p(s, k).start()

        @pl.when(gathers(k))
        def _():
            grad[...] = product(xall[s, k], c_own[s])

        @pl.when(jnp.logical_not(gathers(k)))
        def _():
            at = pl.ds(pl.multiple_of(z * chip_rows, chip_rows), chip_rows)
            grad[...] = product(xall[s, k, at, :], c_own[s, at, :])
            give_p(s, k).wait_recv()
            grad[...] += p_in[s, k].astype(jnp.float32)

    def tiles(body):
        def run(t, carry):
            body(pl.ds(pl.multiple_of(t * TILE, TILE), TILE), t * TILE)
            return carry

        lax.fori_loop(0, width // TILE, run, 0)

    def first_step(k):
        gradient(0, k)

        @pl.when(k == 0)
        def _():
            loads[1].wait()
            loads[2].wait()

        def body(at, low):
            whole = pl.ds(pl.multiple_of(k * width + low, TILE), TILE)
            g = grad[at, :] * factor
            m = 0.1 * g
            v = 0.95 * v_own[whole, :].astype(jnp.float32) + 0.05 * g * g
            u = w_own[whole, :].astype(jnp.float32) - 0.2 * m / (jnp.sqrt(v) + 1e-08)
            u0[k, at, :] = u.astype(jnp.bfloat16)
            first[whole, :] = m.astype(jnp.bfloat16)
            v_own[whole, :] = v.astype(jnp.bfloat16)

        tiles(body)
        swap_a(k).start()

    def second_step(k):
        gradient(1, k)
        swap_a(k).wait_recv()

        def body(at, low):
            whole = pl.ds(pl.multiple_of(k * width + low, TILE), TILE)
            g = grad[at, :] * factor
            m = 0.9 * first[whole, :].astype(jnp.float32) + 0.1 * g
            v = 0.95 * v_own[whole, :].astype(jnp.float32) + 0.05 * g * g
            w = (u0[k, at, :].astype(jnp.float32) + u0_in[k, at, :].astype(jnp.float32)) * 0.5
            w = w.astype(jnp.bfloat16).astype(jnp.float32)
            u = w - 0.2 * m / (jnp.sqrt(v) + 1e-08)
            u1[k, at, :] = u.astype(jnp.bfloat16)

        tiles(body)
        swap_b(k).start()

    def finish(k):
        swap_b(k).wait_recv()

        def body(at, low):
            w = (u1[k, at, :].astype(jnp.float32) + u1_in[k, at, :].astype(jnp.float32)) * 0.5
            out[k, at, :] = w.astype(jnp.bfloat16)

        tiles(body)
        store(k).start()

    def each(i, act):
        @pl.when(jnp.logical_and(i >= 0, i < CHUNKS))
        def _():
            act(0, i)

        @pl.when(jnp.logical_and(i >= LAG, i < CHUNKS + LAG))
        def _():
            act(1, i - LAG)

    def turn(i, carry):
        each(i + AHEAD, send_own)

        if FULL < CHUNKS:

            @pl.when(jnp.logical_and(i == -1, is_end))
            def _():
                give_c(0).start()
                give_c(1).start()

        each(i + 2, partial(pass_on, 1))
        each(i + 1, partial(pass_on, 2))
        each(i, partial(pass_on, 3))

        @pl.when(i == 0)
        def _():
            loads[0].wait()

        @pl.when(jnp.logical_and(i >= 0, i < CHUNKS))
        def _():
            first_step(i)

        @pl.when(jnp.logical_and(i >= LAG, i < CHUNKS + LAG))
        def _():
            second_step(i - LAG)

        @pl.when(i >= LAG + LAST)
        def _():
            finish(i - LAG - LAST)

        each(i - 1, drain)
        return carry

    lax.fori_loop(-AHEAD, CHUNKS + LAG + LAST, turn, 0)

    if FULL < CHUNKS:

        @pl.when(is_end)
        def _():
            give_c(0).wait_send()
            give_c(1).wait_send()

    def finish_sends(k, carry):
        swap_a(k).wait_send()
        swap_b(k).wait_send()
        store(k).wait()
        return carry

    lax.fori_loop(0, CHUNKS, finish_sends, 0)


def run_pair(number, bit_a, bit_b, weight, second, inputs, cotangent):
    _, din, cols = weight.shape
    steps, _, rows, _ = inputs.shape
    total = cotangent.shape[2]
    width = din // CHUNKS
    half = jnp.bfloat16
    piece = (CHUNKS, width, cols)
    dma = pltpu.SemaphoreType.DMA
    return pl.pallas_call(
        partial(gossip_kernel, bit_a, bit_b),
        out_shape=jax.ShapeDtypeStruct(weight.shape, weight.dtype),
        in_specs=[pl.BlockSpec(memory_space=pl.ANY)] * 4,
        out_specs=pl.BlockSpec(memory_space=pl.ANY),
        scratch_shapes=[
            pltpu.VMEM((steps, CHUNKS, total, width), half),
            pltpu.VMEM((din, cols), half),
            pltpu.VMEM((din, cols), half),
            pltpu.VMEM((steps, total, cols), half),
            pltpu.VMEM((steps, total - 2 * rows, cols), half),
            pltpu.VMEM((width, cols), jnp.float32),
            pltpu.VMEM((din, cols), half),
            pltpu.VMEM(piece, half),
            pltpu.VMEM(piece, half),
            pltpu.VMEM(piece, half),
            pltpu.VMEM(piece, half),
            pltpu.VMEM(piece, half),
            pltpu.VMEM((steps,) + piece, half),
            pltpu.VMEM((steps,) + piece, half),
            dma((3,)),
            dma((steps, CHUNKS)),
            dma((4, steps, CHUNKS)),
            dma((4, steps, CHUNKS)),
            dma((4, steps, CHUNKS)),
            dma((4, steps, CHUNKS)),
            dma((4, steps, CHUNKS)),
            dma((2, CHUNKS)),
            dma((2, CHUNKS)),
            dma((2, steps, CHUNKS)),
            dma((2, steps)),
            dma((CHUNKS,)),
        ],
        compiler_params=pltpu.CompilerParams(
            collective_id=number, has_side_effects=True, vmem_limit_bytes=48 << 20
        ),
    )(weight, second, inputs, cotangent)


def per_device(weight, second_moment, inputs, cotangent, gossip_steps):
    top = lax.axis_size("rep").bit_length() - 2
    pairs = [(top, low) for low in range(top)] + [(low, top) for low in range(top)]
    branches = [partial(run_pair, n, a, b) for n, (a, b) in enumerate(pairs)]
    which = jnp.where(gossip_steps[0] == top, gossip_steps[1], top + gossip_steps[0])
    return lax.switch(which, branches, weight, second_moment, inputs, cotangent)


def solution(mesh):
    in_specs = (
        P("rep", None, "tp"),
        P("rep", None, "tp"),
        P(None, "rep", "tp", None),
        P(None, "rep", None, "tp"),
        P(),
    )
    out_specs = P("rep", None, "tp")
    return jax.shard_map(
        per_device, mesh=mesh, in_specs=in_specs, out_specs=out_specs, check_vma=False
    )
```

```python
from functools import partial
import math

import jax
import jax.numpy as jnp
from jax import lax
from jax.experimental import pallas as pl
from jax.experimental.pallas import tpu as pltpu
from jax.sharding import PartitionSpec as P

CHUNKS = 8
FULL = (3, 2)
LAG = 2
LAST = 3
AHEAD = 7
AHEAD_MID = 5
HOPS = (3, 1, 0)
PARTS = 6
TILE = 64
MESH = pl.DeviceIdType.MESH


def gossip_kernel(
    bit_a,
    bit_b,
    w_hbm,
    v_hbm,
    x_hbm,
    c_hbm,
    o_hbm,
    xall,
    w_own,
    v_own,
    c_own,
    c_end,
    grad,
    first,
    u0,
    u0_in,
    u1,
    u1_in,
    out,
    p_out,
    p_in,
    sem_in,
    sem_x,
    recv_n,
    recv_s,
    send_r,
    send_l,
    send_s,
    sem_a,
    sem_b,
    sem_p,
    sem_c,
    sem_o,
):
    rows = x_hbm.shape[2]
    din = x_hbm.shape[3]
    width = xall.shape[3]
    total = xall.shape[2]
    chip_rows = 2 * rows
    rest = total - chip_rows
    factor = 1.0 / math.sqrt(din)

    rep = lax.axis_index("rep")
    tp = lax.axis_index("tp")
    z = tp // 2
    core = tp % 2
    sibling = {"tp": z * 2 + 1 - core}
    right = {"tp": jnp.minimum(tp + 2, 7)}
    left = {"tp": jnp.maximum(tp - 2, 0)}
    at_a, at_b = 1 << bit_a, 1 << bit_b
    mate_a = {"rep": rep + at_a - 2 * at_a * ((rep // at_a) % 2)}
    mate_b = {"rep": rep + at_b - 2 * at_b * ((rep // at_b) % 2)}
    is_first = z == 0
    is_last = z == 3
    is_end = jnp.logical_or(is_first, is_last)
    is_mid = jnp.logical_not(is_end)
    inner = {"tp": jnp.where(is_first, 2 + core, 4 + core)}
    outer = {"tp": jnp.where(z == 1, core, 6 + core)}

    count = 2 * CHUNKS

    def unit(n):
        j = (n - LAG) // 2
        odd = (n - LAG) % 2
        lead, trail = n < LAG, n >= count - LAG
        step = jnp.where(lead, 0, jnp.where(trail, 1, odd))
        piece = jnp.where(odd == 1, j, LAG + j)
        return step, jnp.where(lead, n, jnp.where(trail, n - CHUNKS, piece))

    x_rows = pl.ds(pl.multiple_of(tp * rows, rows), rows)

    def load_x(s, k):
        cols = pl.ds(pl.multiple_of(k * width, width), width)
        return pltpu.make_async_copy(
            x_hbm.at[s, 0, :, cols], xall.at[s, k, x_rows, :], sem_x.at[s, k]
        )

    loads = [
        pltpu.make_async_copy(c_hbm.at[:, 0], c_own, sem_in.at[0]),
        pltpu.make_async_copy(w_hbm.at[0], w_own, sem_in.at[1]),
        pltpu.make_async_copy(v_hbm.at[0], v_own, sem_in.at[2]),
    ]

    def start_x(k, carry):
        load_x(0, k).start()
        load_x(1, k).start()
        return carry

    lax.fori_loop(0, CHUNKS, start_x, 0)
    for load in loads:
        load.start()

    barrier = pltpu.get_barrier_semaphore()
    for mate in (sibling, mate_a, mate_b):
        pl.semaphore_signal(barrier, inc=1, device_id=mate, device_id_type=MESH)

    @pl.when(z < 3)
    def _():
        pl.semaphore_signal(barrier, inc=1, device_id=right, device_id_type=MESH)

    @pl.when(z > 0)
    def _():
        pl.semaphore_signal(barrier, inc=1, device_id=left, device_id_type=MESH)

    pl.semaphore_wait(barrier, jnp.where(is_end, 4, 5))

    def block(s, k, source):
        at = pl.ds(pl.multiple_of((source * 2 + core) * rows, rows), rows)
        return xall.at[s, k, at, :]

    def hop(s, k, source, send, recv, to):
        return pltpu.make_async_remote_copy(
            src_ref=block(s, k, source),
            dst_ref=block(s, k, source),
            send_sem=send.at[source, s, k],
            recv_sem=recv.at[source, s, k],
            device_id=to,
            device_id_type=MESH,
        )

    def to_right(s, k, source):
        return hop(s, k, source, send_r, recv_n, right)

    def to_left(s, k, source):
        return hop(s, k, source, send_l, recv_n, left)

    def to_sibling(s, k, source):
        return hop(s, k, source, send_s, recv_s, sibling)

    def whole(s, k):
        return k < jnp.where(s == 0, FULL[0], FULL[1])

    def goes_right(s, k):
        return jnp.logical_or(z < 2, jnp.logical_and(z == 2, whole(s, k)))

    def goes_left(s, k):
        return jnp.logical_or(z > 1, jnp.logical_and(z == 1, whole(s, k)))

    def gathers(s, k):
        return jnp.logical_or(is_mid, whole(s, k))

    def splits(s, k):
        return jnp.logical_not(whole(s, k))

    def give_c(s, q):
        at = pl.ds(pl.multiple_of(q * rows, rows), rows)
        low = jnp.where(is_first, chip_rows, 0)
        return pltpu.make_async_remote_copy(
            src_ref=c_hbm.at[s, 0, pl.ds(pl.multiple_of(low + q * rows, rows), rows), :],
            dst_ref=c_end.at[s, at, :],
            send_sem=sem_c.at[0, s, q],
            recv_sem=sem_c.at[1, s, q],
            device_id=inner,
            device_id_type=MESH,
        )

    def give_p(s, k):
        return pltpu.make_async_remote_copy(
            src_ref=p_out.at[s, k],
            dst_ref=p_in.at[s, k],
            send_sem=sem_p.at[0, s, k],
            recv_sem=sem_p.at[1, s, k],
            device_id=outer,
            device_id_type=MESH,
        )

    def swap(k, mine, theirs, sems, mate):
        return pltpu.make_async_remote_copy(
            src_ref=mine.at[k],
            dst_ref=theirs.at[k],
            send_sem=sems.at[0, k],
            recv_sem=sems.at[1, k],
            device_id=mate,
            device_id_type=MESH,
        )

    def swap_a(k):
        return swap(k, u0, u0_in, sem_a, mate_a)

    def swap_b(k):
        return swap(k, u1, u1_in, sem_b, mate_b)

    def store(k):
        at = pl.ds(pl.multiple_of(k * width, width), width)
        return pltpu.make_async_copy(out.at[k], o_hbm.at[0, at, :], sem_o.at[k])

    def send_own(s, k):
        load_x(s, k).wait()

        @pl.when(goes_right(s, k))
        def _():
            to_right(s, k, z).start()

        @pl.when(goes_left(s, k))
        def _():
            to_left(s, k, z).start()

        to_sibling(s, k, z).start()

    def pass_on(apart, s, k):
        @pl.when(jnp.logical_and(z >= apart, gathers(s, k)))
        def _():
            source = z - apart
            to_right(s, k, source).wait_recv()

            @pl.when(goes_right(s, k))
            def _():
                to_right(s, k, source).start()

            to_sibling(s, k, source).start()

        @pl.when(jnp.logical_and(z + apart <= 3, gathers(s, k)))
        def _():
            source = z + apart
            to_left(s, k, source).wait_recv()

            @pl.when(goes_left(s, k))
            def _():
                to_left(s, k, source).start()

            to_sibling(s, k, source).start()

    def drain(s, k):
        for source in range(4):
            has = jnp.logical_or(z == source, gathers(s, k))

            @pl.when(jnp.logical_and(z >= source, jnp.logical_and(has, goes_right(s, k))))
            def _():
                to_right(s, k, source).wait_send()

            @pl.when(jnp.logical_and(z <= source, jnp.logical_and(has, goes_left(s, k))))
            def _():
                to_left(s, k, source).wait_send()

            @pl.when(has)
            def _():
                to_sibling(s, k, source).wait_send()

        @pl.when(jnp.logical_and(is_mid, splits(s, k)))
        def _():
            give_p(s, k).wait_send()

    def product(x, c):
        return lax.dot_general(
            x, c, (((0,), (0,)), ((), ())), preferred_element_type=jnp.float32
        )

    def gradient(s, k):
        for source in range(4):

            @pl.when(jnp.logical_or(z == source, gathers(s, k)))
            def _():
                to_sibling(s, k, source).wait_recv()

        @pl.when(jnp.logical_and(is_mid, splits(s, k)))
        def _():
            @pl.when(k == jnp.where(s == 0, FULL[0], FULL[1]))
            def _():
                for q in range(PARTS):
                    give_c(s, q).wait_recv()

            at = pl.ds(pl.multiple_of(jnp.where(z == 1, chip_rows, 0), chip_rows), rest)
            p_out[s, k] = product(xall[s, k, at, :], c_end[s]).astype(jnp.bfloat16)
            give_p(s, k).start()

        @pl.when(gathers(s, k))
        def _():
            grad[...] = product(xall[s, k], c_own[s])

        @pl.when(jnp.logical_not(gathers(s, k)))
        def _():
            at = pl.ds(pl.multiple_of(z * chip_rows, chip_rows), chip_rows)
            grad[...] = product(xall[s, k, at, :], c_own[s, at, :])
            give_p(s, k).wait_recv()
            grad[...] += p_in[s, k].astype(jnp.float32)

    def tiles(body):
        def run(t, carry):
            body(pl.ds(pl.multiple_of(t * TILE, TILE), TILE), t * TILE)
            return carry

        lax.fori_loop(0, width // TILE, run, 0)

    def first_step(k):
        @pl.when(k == 0)
        def _():
            loads[1].wait()
            loads[2].wait()

        def body(at, low):
            rows_at = pl.ds(pl.multiple_of(k * width + low, TILE), TILE)
            g = grad[at, :] * factor
            m = 0.1 * g
            v = 0.95 * v_own[rows_at, :].astype(jnp.float32) + 0.05 * g * g
            u = w_own[rows_at, :].astype(jnp.float32) - 0.2 * m / (jnp.sqrt(v) + 1e-08)
            u0[k, at, :] = u.astype(jnp.bfloat16)
            first[rows_at, :] = m.astype(jnp.bfloat16)
            v_own[rows_at, :] = v.astype(jnp.bfloat16)

        tiles(body)
        swap_a(k).start()

    def second_step(k):
        swap_a(k).wait_recv()

        def body(at, low):
            rows_at = pl.ds(pl.multiple_of(k * width + low, TILE), TILE)
            g = grad[at, :] * factor
            m = 0.9 * first[rows_at, :].astype(jnp.float32) + 0.1 * g
            v = 0.95 * v_own[rows_at, :].astype(jnp.float32) + 0.05 * g * g
            w = (u0[k, at, :].astype(jnp.float32) + u0_in[k, at, :].astype(jnp.float32)) * 0.5
            w = w.astype(jnp.bfloat16).astype(jnp.float32)
            u = w - 0.2 * m / (jnp.sqrt(v) + 1e-08)
            u1[k, at, :] = u.astype(jnp.bfloat16)

        tiles(body)
        swap_b(k).start()

    def finish(k):
        swap_b(k).wait_recv()

        def body(at, low):
            w = (u1[k, at, :].astype(jnp.float32) + u1_in[k, at, :].astype(jnp.float32)) * 0.5
            out[k, at, :] = w.astype(jnp.bfloat16)

        tiles(body)
        store(k).start()

    def each(n, act, also=True):
        @pl.when(jnp.logical_and(jnp.logical_and(n >= 0, n < count), also))
        def _():
            act(*unit(n))

    def consume(s, k):
        gradient(s, k)

        @pl.when(s == 0)
        def _():
            first_step(k)

        @pl.when(s == 1)
        def _():
            second_step(k)

    def average(s, k):
        @pl.when(s == 1)
        def _():
            finish(k)

    def turn(n, carry):
        each(n + AHEAD, send_own, is_end)

        @pl.when(jnp.logical_and(is_end, n + AHEAD < PARTS))
        def _():
            for h in range(2):
                q = 2 * (n + AHEAD) + h
                give_c(q // PARTS, q % PARTS).start()

        each(n + AHEAD_MID, send_own, is_mid)
        for apart, early in enumerate(HOPS):
            each(n + early, partial(pass_on, apart + 1))

        @pl.when(n == 0)
        def _():
            loads[0].wait()

        each(n, consume)
        each(n - LAST, average)
        each(n - 2, drain)
        return carry

    lax.fori_loop(-AHEAD, count + LAST, turn, 0)

    @pl.when(is_end)
    def _():
        def finish_c(q, carry):
            give_c(q // PARTS, q % PARTS).wait_send()
            return carry

        lax.fori_loop(0, 2 * PARTS, finish_c, 0)

    def finish_sends(k, carry):
        swap_a(k).wait_send()
        swap_b(k).wait_send()
        store(k).wait()
        return carry

    lax.fori_loop(0, CHUNKS, finish_sends, 0)


def run_pair(number, bit_a, bit_b, weight, second, inputs, cotangent):
    _, din, cols = weight.shape
    steps, _, rows, _ = inputs.shape
    total = cotangent.shape[2]
    width = din // CHUNKS
    half = jnp.bfloat16
    piece = (CHUNKS, width, cols)
    dma = pltpu.SemaphoreType.DMA
    return pl.pallas_call(
        partial(gossip_kernel, bit_a, bit_b),
        out_shape=jax.ShapeDtypeStruct(weight.shape, weight.dtype),
        in_specs=[pl.BlockSpec(memory_space=pl.ANY)] * 4,
        out_specs=pl.BlockSpec(memory_space=pl.ANY),
        scratch_shapes=[
            pltpu.VMEM((steps, CHUNKS, total, width), half),
            pltpu.VMEM((din, cols), half),
            pltpu.VMEM((din, cols), half),
            pltpu.VMEM((steps, total, cols), half),
            pltpu.VMEM((steps, total - 2 * rows, cols), half),
            pltpu.VMEM((width, cols), jnp.float32),
            pltpu.VMEM((din, cols), half),
            pltpu.VMEM(piece, half),
            pltpu.VMEM(piece, half),
            pltpu.VMEM(piece, half),
            pltpu.VMEM(piece, half),
            pltpu.VMEM(piece, half),
            pltpu.VMEM((steps,) + piece, half),
            pltpu.VMEM((steps,) + piece, half),
            dma((3,)),
            dma((steps, CHUNKS)),
            dma((4, steps, CHUNKS)),
            dma((4, steps, CHUNKS)),
            dma((4, steps, CHUNKS)),
            dma((4, steps, CHUNKS)),
            dma((4, steps, CHUNKS)),
            dma((2, CHUNKS)),
            dma((2, CHUNKS)),
            dma((2, steps, CHUNKS)),
            dma((2, steps, PARTS)),
            dma((CHUNKS,)),
        ],
        compiler_params=pltpu.CompilerParams(
            collective_id=number, has_side_effects=True, vmem_limit_bytes=48 << 20
        ),
    )(weight, second, inputs, cotangent)


def per_device(weight, second_moment, inputs, cotangent, gossip_steps):
    top = lax.axis_size("rep").bit_length() - 2
    pairs = [(top, low) for low in range(top)] + [(low, top) for low in range(top)]
    branches = [partial(run_pair, n, a, b) for n, (a, b) in enumerate(pairs)]
    which = jnp.where(gossip_steps[0] == top, gossip_steps[1], top + gossip_steps[0])
    return lax.switch(which, branches, weight, second_moment, inputs, cotangent)


def solution(mesh):
    in_specs = (
        P("rep", None, "tp"),
        P("rep", None, "tp"),
        P(None, "rep", "tp", None),
        P(None, "rep", None, "tp"),
        P(),
    )
    out_specs = P("rep", None, "tp")
    return jax.shard_map(
        per_device, mesh=mesh, in_specs=in_specs, out_specs=out_specs, check_vma=False
    )
```

```python
from functools import partial
import math

import jax
import jax.numpy as jnp
from jax import lax
from jax.experimental import pallas as pl
from jax.experimental.pallas import tpu as pltpu
from jax.sharding import PartitionSpec as P

CHUNKS = 8
FULL = (4, 3)
LAG = 3
LAST = 3
AHEAD = 7
AHEAD_MID = 5
HOPS = (3, 1, 0)
PARTS = 6
TILE = 64
MESH = pl.DeviceIdType.MESH


def gossip_kernel(
    bit_a,
    bit_b,
    w_hbm,
    v_hbm,
    x_hbm,
    c_hbm,
    o_hbm,
    xall,
    w_own,
    v_own,
    c_own,
    c_end,
    grad,
    first,
    u0,
    u0_in,
    u1,
    u1_in,
    out,
    p_out,
    p_in,
    sem_in,
    sem_x,
    recv_n,
    recv_s,
    send_r,
    send_l,
    send_s,
    sem_a,
    sem_b,
    sem_p,
    sem_c,
    sem_o,
):
    rows = x_hbm.shape[2]
    din = x_hbm.shape[3]
    width = xall.shape[3]
    total = xall.shape[2]
    chip_rows = 2 * rows
    rest = total - chip_rows
    factor = 1.0 / math.sqrt(din)

    rep = lax.axis_index("rep")
    tp = lax.axis_index("tp")
    z = tp // 2
    core = tp % 2
    sibling = {"tp": z * 2 + 1 - core}
    right = {"tp": jnp.minimum(tp + 2, 7)}
    left = {"tp": jnp.maximum(tp - 2, 0)}
    at_a, at_b = 1 << bit_a, 1 << bit_b
    mate_a = {"rep": rep + at_a - 2 * at_a * ((rep // at_a) % 2)}
    mate_b = {"rep": rep + at_b - 2 * at_b * ((rep // at_b) % 2)}
    is_first = z == 0
    is_last = z == 3
    is_end = jnp.logical_or(is_first, is_last)
    is_mid = jnp.logical_not(is_end)
    inner = {"tp": jnp.where(is_first, 2 + core, 4 + core)}
    outer = {"tp": jnp.where(z == 1, core, 6 + core)}

    count = 2 * CHUNKS

    def unit(n):
        j = (n - LAG) // 2
        odd = (n - LAG) % 2
        lead, trail = n < LAG, n >= count - LAG
        step = jnp.where(lead, 0, jnp.where(trail, 1, odd))
        piece = jnp.where(odd == 1, j, LAG + j)
        return step, jnp.where(lead, n, jnp.where(trail, n - CHUNKS, piece))

    x_rows = pl.ds(pl.multiple_of(tp * rows, rows), rows)

    def load_x(s, k):
        cols = pl.ds(pl.multiple_of(k * width, width), width)
        return pltpu.make_async_copy(
            x_hbm.at[s, 0, :, cols], xall.at[s, k, x_rows, :], sem_x.at[s, k]
        )

    loads = [
        pltpu.make_async_copy(c_hbm.at[:, 0], c_own, sem_in.at[0]),
        pltpu.make_async_copy(w_hbm.at[0], w_own, sem_in.at[1]),
        pltpu.make_async_copy(v_hbm.at[0], v_own, sem_in.at[2]),
    ]

    def start_x(k, carry):
        load_x(0, k).start()
        load_x(1, k).start()
        return carry

    lax.fori_loop(0, CHUNKS, start_x, 0)
    for load in loads:
        load.start()

    barrier = pltpu.get_barrier_semaphore()
    for mate in (sibling, mate_a, mate_b):
        pl.semaphore_signal(barrier, inc=1, device_id=mate, device_id_type=MESH)

    @pl.when(z < 3)
    def _():
        pl.semaphore_signal(barrier, inc=1, device_id=right, device_id_type=MESH)

    @pl.when(z > 0)
    def _():
        pl.semaphore_signal(barrier, inc=1, device_id=left, device_id_type=MESH)

    pl.semaphore_wait(barrier, jnp.where(is_end, 4, 5))

    def block(s, k, source):
        at = pl.ds(pl.multiple_of((source * 2 + core) * rows, rows), rows)
        return xall.at[s, k, at, :]

    def hop(s, k, source, send, recv, to):
        return pltpu.make_async_remote_copy(
            src_ref=block(s, k, source),
            dst_ref=block(s, k, source),
            send_sem=send.at[source, s, k],
            recv_sem=recv.at[source, s, k],
            device_id=to,
            device_id_type=MESH,
        )

    def to_right(s, k, source):
        return hop(s, k, source, send_r, recv_n, right)

    def to_left(s, k, source):
        return hop(s, k, source, send_l, recv_n, left)

    def to_sibling(s, k, source):
        return hop(s, k, source, send_s, recv_s, sibling)

    def whole(s, k):
        return k < jnp.where(s == 0, FULL[0], FULL[1])

    def goes_right(s, k):
        return jnp.logical_or(z < 2, jnp.logical_and(z == 2, whole(s, k)))

    def goes_left(s, k):
        return jnp.logical_or(z > 1, jnp.logical_and(z == 1, whole(s, k)))

    def gathers(s, k):
        return jnp.logical_or(is_mid, whole(s, k))

    def splits(s, k):
        return jnp.logical_not(whole(s, k))

    def give_c(s, q):
        at = pl.ds(pl.multiple_of(q * rows, rows), rows)
        low = jnp.where(is_first, chip_rows, 0)
        return pltpu.make_async_remote_copy(
            src_ref=c_hbm.at[s, 0, pl.ds(pl.multiple_of(low + q * rows, rows), rows), :],
            dst_ref=c_end.at[s, at, :],
            send_sem=sem_c.at[0, s, q],
            recv_sem=sem_c.at[1, s, q],
            device_id=inner,
            device_id_type=MESH,
        )

    def give_p(s, k):
        return pltpu.make_async_remote_copy(
            src_ref=p_out.at[s, k],
            dst_ref=p_in.at[s, k],
            send_sem=sem_p.at[0, s, k],
            recv_sem=sem_p.at[1, s, k],
            device_id=outer,
            device_id_type=MESH,
        )

    def swap(k, mine, theirs, sems, mate):
        return pltpu.make_async_remote_copy(
            src_ref=mine.at[k],
            dst_ref=theirs.at[k],
            send_sem=sems.at[0, k],
            recv_sem=sems.at[1, k],
            device_id=mate,
            device_id_type=MESH,
        )

    def swap_a(k):
        return swap(k, u0, u0_in, sem_a, mate_a)

    def swap_b(k):
        return swap(k, u1, u1_in, sem_b, mate_b)

    def store(k):
        at = pl.ds(pl.multiple_of(k * width, width), width)
        return pltpu.make_async_copy(out.at[k], o_hbm.at[0, at, :], sem_o.at[k])

    def send_own(s, k):
        load_x(s, k).wait()

        @pl.when(goes_right(s, k))
        def _():
            to_right(s, k, z).start()

        @pl.when(goes_left(s, k))
        def _():
            to_left(s, k, z).start()

        to_sibling(s, k, z).start()

    def pass_on(apart, s, k):
        @pl.when(jnp.logical_and(z >= apart, gathers(s, k)))
        def _():
            source = z - apart
            to_right(s, k, source).wait_recv()

            @pl.when(goes_right(s, k))
            def _():
                to_right(s, k, source).start()

            to_sibling(s, k, source).start()

        @pl.when(jnp.logical_and(z + apart <= 3, gathers(s, k)))
        def _():
            source = z + apart
            to_left(s, k, source).wait_recv()

            @pl.when(goes_left(s, k))
            def _():
                to_left(s, k, source).start()

            to_sibling(s, k, source).start()

    def drain(s, k):
        for source in range(4):
            has = jnp.logical_or(z == source, gathers(s, k))

            @pl.when(jnp.logical_and(z >= source, jnp.logical_and(has, goes_right(s, k))))
            def _():
                to_right(s, k, source).wait_send()

            @pl.when(jnp.logical_and(z <= source, jnp.logical_and(has, goes_left(s, k))))
            def _():
                to_left(s, k, source).wait_send()

            @pl.when(has)
            def _():
                to_sibling(s, k, source).wait_send()

        @pl.when(jnp.logical_and(is_mid, splits(s, k)))
        def _():
            give_p(s, k).wait_send()

    def product(x, c):
        return lax.dot_general(
            x, c, (((0,), (0,)), ((), ())), preferred_element_type=jnp.float32
        )

    def gradient(s, k):
        for source in range(4):

            @pl.when(jnp.logical_or(z == source, gathers(s, k)))
            def _():
                to_sibling(s, k, source).wait_recv()

        @pl.when(jnp.logical_and(is_mid, splits(s, k)))
        def _():
            @pl.when(k == jnp.where(s == 0, FULL[0], FULL[1]))
            def _():
                for q in range(PARTS):
                    give_c(s, q).wait_recv()

            at = pl.ds(pl.multiple_of(jnp.where(z == 1, chip_rows, 0), chip_rows), rest)
            p_out[s, k] = product(xall[s, k, at, :], c_end[s]).astype(jnp.bfloat16)
            give_p(s, k).start()

        @pl.when(gathers(s, k))
        def _():
            grad[...] = product(xall[s, k], c_own[s])

        @pl.when(jnp.logical_not(gathers(s, k)))
        def _():
            at = pl.ds(pl.multiple_of(z * chip_rows, chip_rows), chip_rows)
            grad[...] = product(xall[s, k, at, :], c_own[s, at, :])
            give_p(s, k).wait_recv()
            grad[...] += p_in[s, k].astype(jnp.float32)

    def tiles(body):
        def run(t, carry):
            body(pl.ds(pl.multiple_of(t * TILE, TILE), TILE), t * TILE)
            return carry

        lax.fori_loop(0, width // TILE, run, 0)

    def first_step(k):
        @pl.when(k == 0)
        def _():
            loads[1].wait()
            loads[2].wait()

        def body(at, low):
            rows_at = pl.ds(pl.multiple_of(k * width + low, TILE), TILE)
            g = grad[at, :] * factor
            m = 0.1 * g
            v = 0.95 * v_own[rows_at, :].astype(jnp.float32) + 0.05 * g * g
            u = w_own[rows_at, :].astype(jnp.float32) - 0.2 * m / (jnp.sqrt(v) + 1e-08)
            u0[k, at, :] = u.astype(jnp.bfloat16)
            first[rows_at, :] = m.astype(jnp.bfloat16)
            v_own[rows_at, :] = v.astype(jnp.bfloat16)

        tiles(body)
        swap_a(k).start()

    def second_step(k):
        swap_a(k).wait_recv()

        def body(at, low):
            rows_at = pl.ds(pl.multiple_of(k * width + low, TILE), TILE)
            g = grad[at, :] * factor
            m = 0.9 * first[rows_at, :].astype(jnp.float32) + 0.1 * g
            v = 0.95 * v_own[rows_at, :].astype(jnp.float32) + 0.05 * g * g
            w = (u0[k, at, :].astype(jnp.float32) + u0_in[k, at, :].astype(jnp.float32)) * 0.5
            w = w.astype(jnp.bfloat16).astype(jnp.float32)
            u = w - 0.2 * m / (jnp.sqrt(v) + 1e-08)
            u1[k, at, :] = u.astype(jnp.bfloat16)

        tiles(body)
        swap_b(k).start()

    def finish(k):
        swap_b(k).wait_recv()

        def body(at, low):
            w = (u1[k, at, :].astype(jnp.float32) + u1_in[k, at, :].astype(jnp.float32)) * 0.5
            out[k, at, :] = w.astype(jnp.bfloat16)

        tiles(body)
        store(k).start()

    def each(n, act, also=True):
        @pl.when(jnp.logical_and(jnp.logical_and(n >= 0, n < count), also))
        def _():
            act(*unit(n))

    def consume(s, k):
        gradient(s, k)

        @pl.when(s == 0)
        def _():
            first_step(k)

        @pl.when(s == 1)
        def _():
            second_step(k)

    def average(s, k):
        @pl.when(s == 1)
        def _():
            finish(k)

    def turn(n, carry):
        each(n + AHEAD, send_own, is_end)

        q = n + AHEAD

        @pl.when(jnp.logical_and(is_end, q < 2 * PARTS))
        def _():
            give_c(q // PARTS, q % PARTS).start()

        each(n + AHEAD_MID, send_own, is_mid)
        for apart, early in enumerate(HOPS):
            each(n + early, partial(pass_on, apart + 1))

        @pl.when(n == 0)
        def _():
            loads[0].wait()

        each(n, consume)
        each(n - LAST, average)
        each(n - 2, drain)
        return carry

    lax.fori_loop(-AHEAD, count + LAST, turn, 0)

    @pl.when(is_end)
    def _():
        def finish_c(q, carry):
            give_c(q // PARTS, q % PARTS).wait_send()
            return carry

        lax.fori_loop(0, 2 * PARTS, finish_c, 0)

    def finish_sends(k, carry):
        swap_a(k).wait_send()
        swap_b(k).wait_send()
        store(k).wait()
        return carry

    lax.fori_loop(0, CHUNKS, finish_sends, 0)


def run_pair(number, bit_a, bit_b, weight, second, inputs, cotangent):
    _, din, cols = weight.shape
    steps, _, rows, _ = inputs.shape
    total = cotangent.shape[2]
    width = din // CHUNKS
    half = jnp.bfloat16
    piece = (CHUNKS, width, cols)
    dma = pltpu.SemaphoreType.DMA
    return pl.pallas_call(
        partial(gossip_kernel, bit_a, bit_b),
        out_shape=jax.ShapeDtypeStruct(weight.shape, weight.dtype),
        in_specs=[pl.BlockSpec(memory_space=pl.ANY)] * 4,
        out_specs=pl.BlockSpec(memory_space=pl.ANY),
        scratch_shapes=[
            pltpu.VMEM((steps, CHUNKS, total, width), half),
            pltpu.VMEM((din, cols), half),
            pltpu.VMEM((din, cols), half),
            pltpu.VMEM((steps, total, cols), half),
            pltpu.VMEM((steps, total - 2 * rows, cols), half),
            pltpu.VMEM((width, cols), jnp.float32),
            pltpu.VMEM((din, cols), half),
            pltpu.VMEM(piece, half),
            pltpu.VMEM(piece, half),
            pltpu.VMEM(piece, half),
            pltpu.VMEM(piece, half),
            pltpu.VMEM(piece, half),
            pltpu.VMEM((steps,) + piece, half),
            pltpu.VMEM((steps,) + piece, half),
            dma((3,)),
            dma((steps, CHUNKS)),
            dma((4, steps, CHUNKS)),
            dma((4, steps, CHUNKS)),
            dma((4, steps, CHUNKS)),
            dma((4, steps, CHUNKS)),
            dma((4, steps, CHUNKS)),
            dma((2, CHUNKS)),
            dma((2, CHUNKS)),
            dma((2, steps, CHUNKS)),
            dma((2, steps, PARTS)),
            dma((CHUNKS,)),
        ],
        compiler_params=pltpu.CompilerParams(
            collective_id=number, has_side_effects=True, vmem_limit_bytes=48 << 20
        ),
    )(weight, second, inputs, cotangent)


def per_device(weight, second_moment, inputs, cotangent, gossip_steps):
    top = lax.axis_size("rep").bit_length() - 2
    pairs = [(top, low) for low in range(top)] + [(low, top) for low in range(top)]
    branches = [partial(run_pair, n, a, b) for n, (a, b) in enumerate(pairs)]
    which = jnp.where(gossip_steps[0] == top, gossip_steps[1], top + gossip_steps[0])
    return lax.switch(which, branches, weight, second_moment, inputs, cotangent)


def solution(mesh):
    in_specs = (
        P("rep", None, "tp"),
        P("rep", None, "tp"),
        P(None, "rep", "tp", None),
        P(None, "rep", None, "tp"),
        P(),
    )
    out_specs = P("rep", None, "tp")
    return jax.shard_map(
        per_device, mesh=mesh, in_specs=in_specs, out_specs=out_specs, check_vma=False
    )
```
